256 devices in a mesh: dp: 16 (over x, z_lo, core), seq: 16 (over y, z_hi).
Axes of the slice: x: 4, y: 4, z: 8 (z_hi: 4, z_lo: 2; z = z_hi * 2 + z_lo), core: 2. Of those that a mesh axis runs over, the one named last changes fastest.
Arguments:
- query_in: bfloat16 [512, 262144], P('dp', 'seq'), may hold values from -6 to 6
- key_in: bfloat16 [512, 262144], P('dp', 'seq'), may hold values from -6 to 6
- values_in: bfloat16 [512, 262144], P('dp', 'seq'), may hold values from -6 to 6
- kernel: bfloat16 [512, 262144], P('dp', 'seq'), may hold values from -6 to 6
- cotangent: bfloat16 [512, 262144], P('dp', 'seq'), may hold values from -6 to 6
- right_in: bfloat16 [512, 512], P('dp'), may hold values from -0.25 to 0.25
- left_in: bfloat16 [512, 512], P('dp'), may hold values from -0.25 to 0.25
- right_out: bfloat16 [512, 512], P('dp'), may hold values from -0.25 to 0.25
- left_out: bfloat16 [512, 512], P('dp'), may hold values from -0.25 to 0.25
- twiddle_one: float32 [512, 512], P(None, 'seq'), may hold values from 0.5 to 2
- twiddle_two: float32 [512, 512], P(None, 'seq'), may hold values from 0.5 to 2
Outputs:
- mixed_out: bfloat16 [512, 262144], P('dp', 'seq')
- grad_query: bfloat16 [512, 262144], P('dp', 'seq')
- grad_key: bfloat16 [512, 262144], P('dp', 'seq')
- grad_value: bfloat16 [512, 262144], P('dp', 'seq')
- grad_kernel: bfloat16 [512, 262144], P('dp', 'seq')
- grad_right_in: float32 [512, 512], P('dp')
- grad_left_in: float32 [512, 512], P('dp')
- grad_right_out: float32 [512, 512], P('dp')
- grad_left_out: float32 [512, 512], P('dp')
The draws below stay inside these ranges and needn't reach their ends.
All inputs are finite; a program needn't handle non-finite values.
Results may differ from the reference program's by a relative error of at most 0.03.
Values may be sent and summed in bfloat16 or wider, within the bound.
A program may use at most 128 MiB of HBM per device.

```python
import math
import jax
import jax.numpy as jnp
from jax import lax

C = 512
NB = 512
BS = 512
L = 262144
N_DP = 16


def level_of(own_key, extent, shards, least, largest):
    loudness, own = 1.0, jax.random.fold_in(own_key, 6)
    for position, blocks in shards:
        draws = jnp.exp(jax.random.uniform(jax.random.fold_in(own, position), (blocks,), jnp.float32, least / len(shards), largest / len(shards)))
        loudness = loudness * jnp.repeat(draws, extent[position] // blocks).reshape([-1 if axis == position else 1 for axis in range(len(extent))])
    return loudness


def bell_draw(rng, dims, deviation, reach, pieces=(), dtype=jnp.bfloat16):
    values = deviation * jax.random.normal(rng, dims, jnp.float32)
    if pieces:
        values = values * level_of(rng, dims, pieces, -0.22, 0.18)
    return jnp.clip(values, -reach, reach).astype(dtype)


def setup_inputs(seed: int = 0) -> dict:
    streams_of = jax.random.split(jax.random.key(seed), 12)
    query_in = bell_draw(streams_of[0], (C, L), 1.0, 6.0, ((0, 16), (1, 16)))
    key_in = bell_draw(streams_of[1], (C, L), 1.0, 6.0, ((0, 16), (1, 16)))
    values_in = bell_draw(streams_of[2], (C, L), 1.0, 6.0, ((0, 16), (1, 16)))
    kernel = bell_draw(streams_of[3], (C, L), 1.0, 6.0, ((0, 16), (1, 16)))
    cotangent = bell_draw(streams_of[4], (C, L), 1.0, 6.0, ((0, 16), (1, 16)))
    right_in = bell_draw(streams_of[5], (BS, BS), BS ** -0.5, 0.25, ((0, 16),))
    left_in = bell_draw(streams_of[6], (NB, NB), NB ** -0.5, 0.25, ((0, 16),))
    right_out = bell_draw(streams_of[7], (NB, NB), NB ** -0.5, 0.25, ((0, 16),))
    left_out = bell_draw(streams_of[8], (BS, BS), BS ** -0.5, 0.25, ((0, 16),))
    twiddle_one = jnp.clip(jnp.exp(math.log(2.0) - 1.3862944 * jax.random.uniform(streams_of[9], (BS, NB), jnp.float32) ** level_of(streams_of[9], (BS, NB), ((1, 16),), -0.2, 0.2)), 0.5, 2.0)
    twiddle_two = jnp.clip(jnp.exp(math.log(2.0) - 1.3862944 * jax.random.uniform(streams_of[10], (NB, BS), jnp.float32) ** level_of(streams_of[10], (NB, BS), ((1, 16),), -0.2, 0.2)), 0.5, 2.0)
    return dict(query_in=query_in, key_in=key_in, values_in=values_in, kernel=kernel, cotangent=cotangent, right_in=right_in, left_in=left_in, right_out=right_out, left_out=left_out, twiddle_one=twiddle_one, twiddle_two=twiddle_two)


def product(form, first, second):
    return jnp.einsum(form, first.astype(jnp.float32), second.astype(jnp.float32))

def one_group(query, key, values, kern, grad_out, right_in, left_in, right_out, left_out, twiddle_one, twiddle_two):
    scale = 1.0 / math.sqrt(C * NB)
    paired = (key.astype(jnp.float32) * values.astype(jnp.float32)).astype(jnp.bfloat16)
    twisted = (product('cij,jk->cki', paired, right_in) * twiddle_one[None]).astype(jnp.bfloat16)
    mixed_one = product('cji,ik->cjk', twisted, left_in)
    weighted = (mixed_one * kern.astype(jnp.float32)).astype(jnp.bfloat16)
    twisted_two = (product('cji,ik->ckj', weighted, right_out) * twiddle_two[None]).astype(jnp.bfloat16)
    mixed_two = product('cij,jk->cik', twisted_two, left_out)
    mixed_out = (query.astype(jnp.float32) * mixed_two).astype(jnp.bfloat16)
    grad_query = (grad_out.astype(jnp.float32) * mixed_two).astype(jnp.bfloat16)
    grad_mixed = (grad_out.astype(jnp.float32) * query.astype(jnp.float32)).astype(jnp.bfloat16)
    grad_lout = product('cij,cik->jk', twisted_two, grad_mixed) * scale
    back_two = product('cik,jk->cji', grad_mixed, left_out).astype(jnp.bfloat16)
    grad_twisted = (back_two.astype(jnp.float32) * jnp.transpose(twiddle_two)[None]).astype(jnp.bfloat16)
    grad_rout = product('cji,cjk->ik', weighted, grad_twisted) * scale
    grad_weighted = product('cjk,ik->cji', grad_twisted, right_out)
    grad_kernel = (grad_weighted * mixed_one).astype(jnp.bfloat16)
    grad_mixed_one = (grad_weighted * kern.astype(jnp.float32)).astype(jnp.bfloat16)
    grad_lin = product('cji,cjk->ik', twisted, grad_mixed_one) * scale
    back_one = product('cjk,ik->cij', grad_mixed_one, left_in).astype(jnp.bfloat16)
    grad_spread = (back_one.astype(jnp.float32) * jnp.transpose(twiddle_one)[None]).astype(jnp.bfloat16)
    grad_rin = product('cij,cik->jk', paired, grad_spread) * scale
    grad_paired = product('cik,jk->cij', grad_spread, right_in)
    grad_key = (grad_paired * values.astype(jnp.float32)).astype(jnp.bfloat16)
    grad_value = (grad_paired * key.astype(jnp.float32)).astype(jnp.bfloat16)
    return (mixed_out, grad_query, grad_key, grad_value, grad_kernel, grad_rin, grad_lin, grad_rout, grad_lout)

def reference(query_in, key_in, values_in, kernel, cotangent, right_in, left_in, right_out, left_out, twiddle_one, twiddle_two):
    groups = N_DP
    width = C // groups

    def split(array, first, second):
        return array.reshape(groups, width, first, second)
    stacked = (split(query_in, NB, BS), split(key_in, NB, BS), split(values_in, NB, BS), split(kernel, BS, NB), split(cotangent, NB, BS))

    def run(item):
        return one_group(item[0], item[1], item[2], item[3], item[4], right_in, left_in, right_out, left_out, twiddle_one, twiddle_two)
    result = lax.map(run, stacked)
    mixed_out = result[0].reshape(C, NB * BS)
    grad_query = result[1].reshape(C, NB * BS)
    grad_key = result[2].reshape(C, NB * BS)
    grad_value = result[3].reshape(C, NB * BS)
    grad_kernel = result[4].reshape(C, NB * BS)
    grad_right_in = lax.optimization_barrier(jnp.sum(result[5], axis=0))
    grad_left_in = lax.optimization_barrier(jnp.sum(result[6], axis=0))
    grad_right_out = lax.optimization_barrier(jnp.sum(result[7], axis=0))
    grad_left_out = lax.optimization_barrier(jnp.sum(result[8], axis=0))
    return (mixed_out, grad_query, grad_key, grad_value, grad_kernel, grad_right_in, grad_left_in, grad_right_out, grad_left_out)
```

```python
import math

import jax
import jax.numpy as jnp
from jax import lax
from jax.experimental import pallas as pl
from jax.experimental.pallas import tpu as pltpu
from jax.sharding import PartitionSpec as P

C = 512
NB = 512
BS = 512
SCALE = 1.0 / math.sqrt(C * NB)
BF = jnp.bfloat16
F32 = jnp.float32
NT = (((1,), (1,)), ((), ()))
NN = (((1,), (0,)), ((), ()))
TN = (((0,), (0,)), ((), ()))
R1, L2, L1, R2 = 0, 1, 2, 3
T1, DT2, T2, DT1 = 0, 1, 2, 3
GRO, GLI, GLO, GRI = 0, 1, 2, 3


def dot(a, b, dims):
    return lax.dot_general(a, b, dims, preferred_element_type=F32)


def mixer(
    q_hbm, k_hbm, v_hbm, h_hbm, g_hbm, rin, lin, rout, lout, tw1, tw2,
    mo_hbm, gq_hbm, gk_hbm, gv_hbm, gh_hbm, gri_out, gli_out, gro_out, glo_out,
    qn, kn, vn, hn, gn,
    us, gos, hs, zs, fac, fact, t1x, wx, ds2x, dzx, t2x, ds1x,
    sbuf, rbuf, perm_in, perm_out, regroup, tw1x, tw2x, tw1t, tw2t, nat,
    gb, gc, xs, xr, zb, zr, yr,
    load_sem, out_sem, fs_sem, fr_sem, as_sem, ar_sem,
    gcs_sem, gcr_sem, xs_sem, xr_sem, zs_sem, zr_sem, ys_sem, yr_sem,
):
    dp = lax.axis_index("dp")
    me = lax.axis_index("seq")
    x, zl, co = dp // 4, (dp // 2) % 2, dp % 2
    y, zh = me // 4, me % 4

    def device(dx, dl, dc, dy, dh):
        return {
            "dp": ((x + dx) % 4) * 4 + ((zl + dl) % 2) * 2 + (co + dc) % 2,
            "seq": ((y + dy) % 4) * 4 + (zh + dh) % 4,
        }

    def remote(src, dst, ssem, rsem, to):
        return pltpu.make_async_remote_copy(
            src_ref=src, dst_ref=dst, send_sem=ssem, recv_sem=rsem,
            device_id=to, device_id_type=pl.DeviceIdType.MESH,
        )

    def load(n, hbm, vmem):
        @pl.loop(0, 32)
        def _(i):
            pltpu.make_async_copy(
                hbm.at[:, pl.ds(pl.multiple_of(i * 512, 512), 512)], vmem.at[i], load_sem.at[n]
            ).start()

    def load_wait(n, vmem):
        pltpu.make_async_copy(vmem, vmem, load_sem.at[n]).wait()

    def store(n, hbm, vmem):
        @pl.loop(0, 32)
        def _(i):
            pltpu.make_async_copy(
                vmem.at[i], hbm.at[:, pl.ds(pl.multiple_of(i * 512, 512), 512)], out_sem.at[n]
            ).start()

    def store_wait(n, vmem):
        pltpu.make_async_copy(vmem, vmem, out_sem.at[n]).wait()

    peers = (
        [(0, 0, 0, dy, dh) for dy in range(4) for dh in range(4) if dy or dh]
        + [(dx, 0, 0, dy, 0) for dx in range(1, 4) for dy in range(4)]
        + [(0, 1, 0, 0, dh) for dh in range(4)]
        + [(0, 0, 1, 0, 0)]
    )
    barrier = pltpu.get_barrier_semaphore()
    for offset in peers:
        pl.semaphore_signal(
            barrier, inc=1, device_id=device(*offset), device_id_type=pl.DeviceIdType.MESH
        )
    load(0, k_hbm, kn)
    load(1, v_hbm, vn)
    load(2, g_hbm, gn)
    load(3, q_hbm, qn)
    load(4, h_hbm, hn)

    def grid2(shape, hold):
        r = lax.broadcasted_iota(jnp.int32, shape, 0)
        q = lax.broadcasted_iota(jnp.int32, shape, 1)
        return jnp.where(hold(r, q), 1.0, 0.0).astype(BF)

    perm_in[...] = grid2((512, 512), lambda r, q: (r >> 4 == (q & 31)) & ((r & 15) == q >> 5))
    pl.semaphore_wait(barrier, len(peers))

    def fcopy(f, block, to):
        return remote(fac.at[f, block], fac.at[f, block], fs_sem.at[f, block, 0], fr_sem.at[f, block], to)

    xpeers = (2, 1, 3)
    zblock = x * 4 + (1 - zl) * 2 + co

    def fsend(f, block, slot, to):
        remote(
            fac.at[f, block], fac.at[f, block], fs_sem.at[f, block, slot], fr_sem.at[f, block], to
        ).start()

    def fwait_send(f, block, slot):
        remote(
            fac.at[f, block], fac.at[f, block], fs_sem.at[f, block, slot], fr_sem.at[f, block],
            device(0, 0, 1, 0, 0),
        ).wait_send()

    def fwait(f, block):
        remote(
            fac.at[f, block], fac.at[f, block], fs_sem.at[f, block, 0], fr_sem.at[f, block],
            device(0, 0, 1, 0, 0),
        ).wait_recv()

    def gather_a(f, ref):
        fac[f, dp] = ref[...]
        fsend(f, dp, 4, device(0, 1, 0, 0, 0))
        for dx in xpeers:
            fsend(f, dp, dx, device(dx, 0, 0, 0, 0))
        fsend(f, dp, 0, device(0, 0, 1, 0, 0))

    def gather_b(f):
        fwait(f, zblock)
        for dx in xpeers:
            fsend(f, zblock, dx, device(dx, 0, 0, 0, 0))
        fsend(f, zblock, 0, device(0, 0, 1, 0, 0))

    def gather_c(f):
        for dl in range(2):
            for dx in (1, 3, 2):
                block = ((x + dx) % 4) * 4 + ((zl + dl) % 2) * 2 + co
                fwait(f, block)
                fsend(f, block, 0, device(0, 0, 1, 0, 0))

    def gather_d(f):
        @pl.loop(0, 8)
        def _(b):
            fwait(f, b * 2 + 1 - co)

    def gather_end(f):
        for dx in xpeers:
            fwait_send(f, dp, dx)
            fwait_send(f, zblock, dx)
        fwait_send(f, dp, 4)

        @pl.loop(0, 8)
        def _(b):
            fwait_send(f, b * 2 + co, 0)

    def factor(f):
        return fac[f].reshape(512, 512)

    def shuffle(src, dst):
        @pl.loop(0, 2)
        def _(n):
            block = src[pl.ds(n * 16, 16)].reshape(512, 512)
            dst[:, pl.ds(pl.multiple_of(n * 16, 16), 16), :] = (
                dot(perm_in[...], block, NN).astype(BF).reshape(32, 16, 512)
            )

    def product(a, b, dst):
        @pl.loop(0, 32)
        def _(i):
            dst[i] = (a[i].astype(F32) * b[i].astype(F32)).astype(BF)

    def exchange_send(n):
        for dy in range(4):
            for dh in (2, 1, 3, 0):
                if dy or dh:
                    to = ((y + dy) % 4) * 4 + (zh + dh) % 4
                    remote(
                        sbuf.at[n, to], rbuf.at[n, me], as_sem.at[n, to], ar_sem.at[n, me],
                        device(0, 0, 0, dy, dh),
                    ).start()
        rbuf[n, me] = sbuf[n, me]

    def exchange_wait_send(n):
        for dy in range(4):
            for dh in (2, 1, 3, 0):
                if dy or dh:
                    to = ((y + dy) % 4) * 4 + (zh + dh) % 4
                    remote(
                        sbuf.at[n, to], rbuf.at[n, me], as_sem.at[n, to], ar_sem.at[n, me],
                        device(0, 0, 0, dy, dh),
                    ).wait_send()

    def exchange_wait_recv(n, dy):
        for dh in (2, 1, 3, 0):
            if dy or dh:
                source = ((y - dy + 4) % 4) * 4 + (zh - dh + 4) % 4
                remote(
                    sbuf.at[n, source], rbuf.at[n, source], as_sem.at[n, source],
                    ar_sem.at[n, source], device(0, 0, 0, dy, dh),
                ).wait_recv()

    def arrange(n, dst, twist):
        for dy in range(4):
            exchange_wait_recv(n, dy)
            yg = (y - dy + 4) % 4
            lhs = jnp.concatenate(
                [
                    jnp.concatenate(
                        [rbuf[n, yg * 4 + b, :, ch * 128 : ch * 128 + 128] for b in range(4)], axis=1
                    )
                    for ch in range(8)
                ],
                axis=0,
            )
            lanes = pl.ds(pl.multiple_of(yg * 128, 128), 128)
            out = dot(lhs, regroup[...], NN)
            for ch in range(8):
                for cl in range(4):
                    piece = out[ch * 32 : ch * 32 + 32, cl * 128 : cl * 128 + 128]
                    if twist is not None:
                        piece = piece * twist[:, lanes]
                    dst[ch * 4 + cl, :, lanes] = piece.astype(BF)

    def spread(n, left, right, twist):
        @pl.loop(0, 4)
        def _(m):
            out = dot(left, right[pl.ds(m * 8, 8)].reshape(256, 512), NT)
            for part in range(2):
                piece = out[:, part * 128 : part * 128 + 128]
                if twist is not None:
                    piece = piece * twist[...]
                lanes = pl.ds(pl.multiple_of(m * 256 + part * 128, 128), 128)
                sbuf[n, :, :, lanes] = piece.astype(BF).reshape(16, 32, 128)

    def share(n, first, second):
        @pl.loop(0, 4)
        def _(m):
            lanes = pl.ds(pl.multiple_of(m * 128, 128), 128)
            out = dot(first[:, :, lanes].reshape(1024, 128), second[...].reshape(1024, 512), TN)
            out = out.astype(BF)
            for p in range(4):
                gb[n, p % 2, m * 2 + p // 2] = out[p * 32 : p * 32 + 32]

    def core_copy(n):
        return remote(
            gb.at[n, 1 - co], gc.at[n], gcs_sem.at[n], gcr_sem.at[n], device(0, 0, 1, 0, 0)
        )

    def core_send(n):
        core_copy(n).start()

    def xy_copy(n, dx, dy):
        to = ((x + dx) % 4) * 4 + (y + dy) % 4
        return remote(
            xs.at[n, to], xr.at[n, x * 4 + y], xs_sem.at[n, to], xr_sem.at[n, x * 4 + y],
            device(dx, 0, 0, dy, 0),
        )

    XY = [(dx, dy) for dx in (2, 1, 3, 0) for dy in (2, 1, 3, 0) if dx or dy]

    def xy_send(n):
        core_copy(n).wait_recv()

        @pl.loop(0, 4)
        def _(m):
            total = gb[n, co, pl.ds(m * 2, 2)].astype(F32) + gc[n, pl.ds(m * 2, 2)].astype(F32)
            total = total.astype(BF).reshape(64, 512)
            for p in range(4):
                xs[n, m * 4 + p] = total[:, p * 128 : p * 128 + 128]

        for dx, dy in XY:
            xy_copy(n, dx, dy).start()
        xr[n, x * 4 + y] = xs[n, x * 4 + y]

    def z_copy(n, dh, dl):
        z = zh * 2 + zl
        to = ((zh + dh) % 4) * 2 + (zl + dl) % 2
        return remote(
            zb.at[n, (zl + dl) % 2], zr.at[n, z], zs_sem.at[n, to], zr_sem.at[n, z],
            device(0, dl, 0, 0, dh),
        )

    Z = [(dh, dl) for dh in (2, 1, 3, 0) for dl in range(2) if dh or dl]

    def z_send(n):
        for dx, dy in XY:
            source = ((x - dx + 4) % 4) * 4 + (y - dy + 4) % 4
            remote(
                xs.at[n, source], xr.at[n, source], xs_sem.at[n, source], xr_sem.at[n, source],
                device(dx, 0, 0, dy, 0),
            ).wait_recv()
        total = xr[n, 0].astype(F32)
        for p in range(1, 16):
            total = total + xr[n, p].astype(F32)
        zb[n] = total.astype(BF).reshape(2, 32, 128)
        for dh, dl in Z:
            z_copy(n, dh, dl).start()
        zr[n, zh * 2 + zl] = zb[n, zl]

    def y_copy(n, dy):
        return remote(
            yr.at[n, y], yr.at[n, y], ys_sem.at[n, dy], yr_sem.at[n, y], device(0, 0, 0, dy, 0)
        )

    def y_send(n):
        for dh, dl in Z:
            source = ((zh - dh + 4) % 4) * 2 + (zl - dl + 2) % 2
            remote(
                zb.at[n, 0], zr.at[n, source], zs_sem.at[n, source], zr_sem.at[n, source],
                device(0, dl, 0, 0, dh),
            ).wait_recv()
        total = zr[n, 0].astype(F32)
        for p in range(1, 8):
            total = total + zr[n, p].astype(F32)
        yr[n, y] = total * SCALE
        for dy in (2, 1, 3):
            y_copy(n, dy).start()

    def finish(n, out):
        for dy in (2, 1, 3):
            source = (y - dy + 4) % 4
            remote(
                yr.at[n, source], yr.at[n, source], ys_sem.at[n, dy], yr_sem.at[n, source],
                device(0, 0, 0, dy, 0),
            ).wait_recv()
        for p in range(4):
            out[:, p * 128 : p * 128 + 128] = yr[n, p]

    def reduce_end(n):
        core_copy(n).wait_send()
        for dx, dy in XY:
            xy_copy(n, dx, dy).wait_send()
        for dh, dl in Z:
            z_copy(n, dh, dl).wait_send()
        for dy in (2, 1, 3):
            y_copy(n, dy).wait_send()

    def outputs(left, f, dims, first, second, swap):
        @pl.loop(0, 2)
        def _(n):
            rows = pl.ds(pl.multiple_of(n * 16, 16), 16)
            out = dot(left[:, rows, :].reshape(512, 512), factor(f), dims).astype(BF)
            nat[...] = dot(perm_out[...], out, NN).reshape(16, 32, 512)

            @pl.loop(0, 16)
            def _(i):
                value = nat[i]
                a = first[n * 16 + i].astype(F32)
                b = second[n * 16 + i].astype(F32)
                first[n * 16 + i] = (value * (b if swap else a)).astype(BF)
                second[n * 16 + i] = (value * (a if swap else b)).astype(BF)

    gather_a(R1, rin)
    load_wait(0, kn)
    load_wait(1, vn)
    product(kn, vn, wx)
    shuffle(wx, us)
    gather_b(R1)
    tw1x[...] = jnp.concatenate([tw1[...]] * 4, axis=1)
    tw2x[...] = jnp.concatenate([tw2[...]] * 4, axis=1)
    gather_c(R1)
    gather_d(R1)
    fact[0] = factor(R1).T
    spread(T1, fact[0], us, tw1x)
    exchange_send(T1)

    for f, ref in ((L2, lout), (L1, lin), (R2, rout)):
        gather_a(f, ref)
    load_wait(2, gn)
    load_wait(3, qn)
    product(gn, qn, wx)
    shuffle(wx, gos)
    for f in (L2, L1, R2):
        gather_b(f)
    regroup[...] = grid2(
        (512, 512),
        lambda r, q: (r >> 7 == ((q >> 5) & 3)) & (((r >> 5) & 3) == q >> 7) & ((r & 31) == (q & 31)),
    )
    perm_out[...] = grid2((512, 512), lambda q, r: (r >> 4 == (q & 31)) & ((r & 15) == q >> 5))
    tw1t[...] = tw1[...].T
    tw2t[...] = tw2[...].T
    for f in (L2, L1, R2):
        gather_c(f)
    load_wait(4, hn)
    shuffle(hn, hs)
    for f in (L2, L1, R2):
        gather_d(f)
    spread(DT2, factor(L2), gos, None)
    fact[1] = factor(R2).T
    exchange_wait_send(T1)
    exchange_send(DT2)

    arrange(T1, t1x, None)

    @pl.loop(0, 4)
    def _(m):
        rows = pl.ds(m * 8, 8)
        out = dot(t1x[rows].reshape(256, 512), factor(L1), NN).reshape(8, 32, 512)
        zs[rows] = out
        wx[rows] = (out * hs[rows].astype(F32)).astype(BF)

    spread(T2, fact[1], wx, tw2x)
    exchange_wait_send(DT2)
    exchange_send(T2)

    arrange(DT2, ds2x, tw2t)

    @pl.loop(0, 2)
    def _(n):
        rows = pl.ds(pl.multiple_of(n * 16, 16), 16)
        out = dot(ds2x[:, rows, :].reshape(512, 512), factor(R2), NT).reshape(32, 16, 512)
        dzx[:, rows, :] = (out * hs[:, rows, :].astype(F32)).astype(BF)
        grad = (out * zs[:, rows, :]).astype(BF).reshape(512, 512)
        hn[pl.ds(n * 16, 16)] = dot(perm_out[...], grad, NN).astype(BF).reshape(16, 32, 512)

    spread(DT1, factor(L1), dzx, None)
    store(4, gh_hbm, hn)
    share(GRO, wx, ds2x)
    core_send(GRO)
    share(GLI, t1x, dzx)
    core_send(GLI)
    xy_send(GRO)
    xy_send(GLI)
    exchange_wait_send(T2)
    exchange_send(DT1)
    z_send(GRO)
    z_send(GLI)

    arrange(T2, t2x, None)
    share(GLO, t2x, gos)
    core_send(GLO)
    outputs(t2x, L2, NN, qn, gn, False)
    store(0, mo_hbm, qn)
    store(1, gq_hbm, gn)
    xy_send(GLO)
    y_send(GRO)
    y_send(GLI)
    z_send(GLO)
    finish(GRO, gro_out)
    finish(GLI, gli_out)
    y_send(GLO)

    arrange(DT1, ds1x, tw1t)
    share(GRI, us, ds1x)
    core_send(GRI)
    finish(GLO, glo_out)
    xy_send(GRI)
    outputs(ds1x, R1, NT, kn, vn, True)
    store(2, gk_hbm, kn)
    store(3, gv_hbm, vn)
    z_send(GRI)
    exchange_wait_send(DT1)
    for f in range(4):
        gather_end(f)
    for n in (GRO, GLI, GLO):
        reduce_end(n)
    y_send(GRI)
    for n, vmem in enumerate((qn, gn, kn, vn, hn)):
        store_wait(n, vmem)
    finish(GRI, gri_out)
    reduce_end(GRI)


def shards(*args):
    any_spec = pl.BlockSpec(memory_space=pl.ANY)
    vmem_spec = pl.BlockSpec(memory_space=pltpu.VMEM)
    stream = pltpu.VMEM((32, 32, 512), BF)
    dma = pltpu.SemaphoreType.DMA
    outs = pl.pallas_call(
        mixer,
        out_shape=[jax.ShapeDtypeStruct((32, 16384), BF)] * 5
        + [jax.ShapeDtypeStruct((32, 512), F32)] * 4,
        in_specs=[any_spec] * 5 + [vmem_spec] * 6,
        out_specs=[any_spec] * 5 + [vmem_spec] * 4,
        scratch_shapes=[stream] * 5
        + [stream] * 3
        + [pltpu.VMEM((32, 32, 512), F32)]
        + [pltpu.VMEM((4, 16, 32, 512), BF), pltpu.VMEM((2, 512, 512), BF)]
        + [stream] * 6
        + [pltpu.VMEM((4, 16, 32, 1024), BF)] * 2
        + [pltpu.VMEM((512, 512), BF)] * 3
        + [pltpu.VMEM((512, 128), F32)] * 2
        + [pltpu.VMEM((32, 512), F32)] * 2
        + [pltpu.VMEM((16, 32, 512), F32)]
        + [
            pltpu.VMEM((4, 2, 8, 32, 512), BF),
            pltpu.VMEM((4, 8, 32, 512), BF),
            pltpu.VMEM((4, 16, 64, 128), BF),
            pltpu.VMEM((4, 16, 64, 128), BF),
            pltpu.VMEM((4, 2, 32, 128), BF),
            pltpu.VMEM((4, 8, 32, 128), BF),
            pltpu.VMEM((4, 4, 32, 128), F32),
        ]
        + [
            dma((5,)), dma((5,)), dma((4, 16, 5)), dma((4, 16)), dma((4, 16)), dma((4, 16)),
            dma((4,)), dma((4,)), dma((4, 16)), dma((4, 16)), dma((4, 8)), dma((4, 8)),
            dma((4, 4)), dma((4, 4)),
        ],
        compiler_params=pltpu.CompilerParams(
            collective_id=0, has_side_effects=True, vmem_limit_bytes=60 << 20
        ),
        cost_estimate=pl.CostEstimate(
            flops=13_000_000_000, bytes_accessed=12 << 20, transcendentals=0
        ),
        name="mixer",
    )(*args)
    return tuple(outs)


def solution(mesh):
    wide, rows, cols = P("dp", "seq"), P("dp", None), P(None, "seq")
    return jax.shard_map(
        shards,
        mesh=mesh,
        in_specs=(wide,) * 5 + (rows,) * 4 + (cols,) * 2,
        out_specs=(wide,) * 5 + (rows,) * 4,
        check_vma=False,
    )
```

```python
import math

import jax
import jax.numpy as jnp
from jax import lax
from jax.experimental import pallas as pl
from jax.experimental.pallas import tpu as pltpu
from jax.sharding import PartitionSpec as P

C = 512
NB = 512
BS = 512
SCALE = 1.0 / math.sqrt(C * NB)
BF = jnp.bfloat16
F32 = jnp.float32
NT = (((1,), (1,)), ((), ()))
NN = (((1,), (0,)), ((), ()))
TN = (((0,), (0,)), ((), ()))
R1, L2, L1, R2 = 0, 1, 2, 3
T1, DT2, T2, DT1 = 0, 1, 2, 3
GRO, GLI, GLO, GRI = 0, 1, 2, 3
WINDOW = 4
YORDER = (1, 2, 3, 0)
PARTS = 4


def dot(a, b, dims):
    return lax.dot_general(a, b, dims, preferred_element_type=F32)


def mixer(
    q_hbm, k_hbm, v_hbm, h_hbm, g_hbm, rin, lin, rout, lout, tw1_hbm, tw2_hbm,
    o_hbm, du_hbm, gh_hbm, grads_hbm,
    qn, kn, vn, hn, gn,
    us, gos, hs, zs, fac, fact, t1x, wx, ds2x, dzx, t2x, ds1x,
    sbuf, rbuf, perm_in, perm_out, regroup, tw1x, tw2x, tw1t, tw2t,
    gb, gc, xs, xr, zb, zr, yr, grads,
    load_sem, own_sem, out_sem, fs_sem, fr_sem, as_sem, ar_sem,
    gcs_sem, gcr_sem, xs_sem, xr_sem, zs_sem, zr_sem, ys_sem, yr_sem,
):
    dp = lax.axis_index("dp")
    me = lax.axis_index("seq")
    x, zl, co = dp // 4, (dp // 2) % 2, dp % 2
    y, zh = me // 4, me % 4

    def device(dx, dl, dc, dy, dh):
        return {
            "dp": ((x + dx) % 4) * 4 + ((zl + dl) % 2) * 2 + (co + dc) % 2,
            "seq": ((y + dy) % 4) * 4 + (zh + dh) % 4,
        }

    def remote(src, dst, ssem, rsem, to):
        return pltpu.make_async_remote_copy(
            src_ref=src, dst_ref=dst, send_sem=ssem, recv_sem=rsem,
            device_id=to, device_id_type=pl.DeviceIdType.MESH,
        )

    def load(n, hbm, vmem):
        @pl.loop(0, 32)
        def _(i):
            pltpu.make_async_copy(
                hbm.at[:, pl.ds(pl.multiple_of(i * 512, 512), 512)], vmem.at[i], load_sem.at[n]
            ).start()

    def load_wait(n, vmem):
        pltpu.make_async_copy(vmem, vmem, load_sem.at[n]).wait()

    def store(n, hbm, vmem):
        @pl.loop(0, 32)
        def _(i):
            pltpu.make_async_copy(
                vmem.at[i], hbm.at[:, pl.ds(pl.multiple_of(i * 512, 512), 512)], out_sem.at[n]
            ).start()

    def store_wait(n, vmem):
        pltpu.make_async_copy(vmem, vmem, out_sem.at[n]).wait()

    peers = (
        [(0, 0, 0, dy, dh) for dy in range(4) for dh in range(4) if dy or dh]
        + [(dx, 0, 0, dy, 0) for dx in range(1, 4) for dy in range(4)]
        + [(0, 1, 0, 0, dh) for dh in range(4)]
        + [(dx, 1, 0, 0, 0) for dx in range(1, 4)]
        + [(0, 0, 1, 0, 0)]
    )
    barrier = pltpu.get_barrier_semaphore()
    for offset in peers:
        pl.semaphore_signal(
            barrier, inc=1, device_id=device(*offset), device_id_type=pl.DeviceIdType.MESH
        )
    own = (rin, lout, lin, rout)
    twist_loads = (
        pltpu.make_async_copy(tw1_hbm, tw1t, own_sem.at[4]),
        pltpu.make_async_copy(tw2_hbm, tw2t, own_sem.at[5]),
    )
    for f in range(4):
        pltpu.make_async_copy(own[f], fac.at[f, dp], own_sem.at[f]).start()
    load(0, k_hbm, kn)
    load(1, v_hbm, vn)
    for copy in twist_loads:
        copy.start()
    load(2, g_hbm, gn)
    load(3, q_hbm, qn)
    load(4, h_hbm, hn)

    def grid2(shape, hold):
        r = lax.broadcasted_iota(jnp.int32, shape, 0)
        q = lax.broadcasted_iota(jnp.int32, shape, 1)
        return jnp.where(hold(r, q), 1.0, 0.0).astype(BF)

    perm_in[...] = grid2((512, 512), lambda r, q: (r >> 4 == (q & 31)) & ((r & 15) == q >> 5))
    pl.semaphore_wait(barrier, len(peers))

    CORE = device(0, 0, 1, 0, 0)
    zblock = x * 4 + (1 - zl) * 2 + co

    def fsend(f, block, slot, to):
        remote(fac.at[f, block], fac.at[f, block], fs_sem.at[0], fr_sem.at[f, slot], to).start()

    def fwait(f, slot, count):
        blocks = fac.at[f, pl.ds(0, count)]
        remote(blocks, blocks, fs_sem.at[0], fr_sem.at[f, slot], CORE).wait_recv()

    def fslot(dx):
        return 1 + dx

    def gather_a(f, direct):
        pltpu.make_async_copy(own[f], fac.at[f, dp], own_sem.at[f]).wait()
        fsend(f, dp, fslot(0), device(0, 1, 0, 0, 0))
        for dx in (2, 1, 3):
            fsend(f, dp, fslot(dx), device(dx, 0, 0, 0, 0))
            if direct:
                fsend(f, dp, fslot(dx), device(dx, 1, 0, 0, 0))
        fsend(f, dp, 0, CORE)

    def gather_b(f, direct):
        fwait(f, fslot(0), 1)
        if not direct:
            for dx in (2, 1, 3):
                fsend(f, zblock, fslot(dx), device(dx, 0, 0, 0, 0))
        fsend(f, zblock, 0, CORE)

    def gather_c(f):
        for dx in (1, 3, 2):
            fwait(f, fslot(dx), 2)
            for side in range(2):
                fsend(f, ((x - dx + 4) % 4) * 4 + side * 2 + co, 0, CORE)

    def gather_d(f):
        fwait(f, 0, 8)

    def gather_end():
        blocks = fac.at[:, pl.ds(0, 15)]
        remote(blocks, blocks, fs_sem.at[0], fr_sem.at[0, 0], CORE).wait_send()

    def factor(f):
        return fac[f].reshape(512, 512)

    def shuffle(src, dst):
        @pl.loop(0, 2)
        def _(n):
            block = src[pl.ds(n * 16, 16)].reshape(512, 512)
            dst[:, pl.ds(pl.multiple_of(n * 16, 16), 16), :] = (
                dot(perm_in[...], block, NN).astype(BF).reshape(32, 16, 512)
            )

    def product(a, b, dst):
        @pl.loop(0, 32)
        def _(i):
            dst[i] = (a[i].astype(F32) * b[i].astype(F32)).astype(BF)

    pending = []

    def exchange_group(dy):
        return [(dy, dh) for dh in (2, 1, 3, 0) if dy or dh]

    def exchange_wait_send(n, dy):
        blocks = sbuf.at[n, pl.ds(0, len(exchange_group(dy)))]
        remote(blocks, blocks, as_sem.at[n, dy], ar_sem.at[n, dy], CORE).wait_send()

    def exchange_send(n):
        rbuf[n, me] = sbuf[n, me]
        for dy in YORDER:
            if len(pending) == WINDOW:
                exchange_wait_send(*pending.pop(0))
            for _, dh in exchange_group(dy):
                to = ((y + dy) % 4) * 4 + (zh + dh) % 4
                remote(
                    sbuf.at[n, to], rbuf.at[n, me], as_sem.at[n, dy], ar_sem.at[n, dy],
                    device(0, 0, 0, dy, dh),
                ).start()
            pending.append((n, dy))

    def exchange_end():
        while pending:
            exchange_wait_send(*pending.pop(0))

    def exchange_wait_recv(n, dy):
        blocks = rbuf.at[n, pl.ds(0, len(exchange_group(dy)))]
        remote(blocks, blocks, as_sem.at[n, dy], ar_sem.at[n, dy], CORE).wait_recv()

    def arrange(n, dst, twist):
        for dy in YORDER:
            exchange_wait_recv(n, dy)
            yg = (y - dy + 4) % 4
            lhs = jnp.concatenate(
                [
                    jnp.concatenate(
                        [rbuf[n, yg * 4 + b, :, ch * 128 : ch * 128 + 128] for b in range(4)], axis=1
                    )
                    for ch in range(8)
                ],
                axis=0,
            )
            lanes = pl.ds(pl.multiple_of(yg * 128, 128), 128)
            out = dot(lhs, regroup[...], NN)
            for ch in range(8):
                for cl in range(4):
                    piece = out[ch * 32 : ch * 32 + 32, cl * 128 : cl * 128 + 128]
                    if twist is not None:
                        piece = piece * twist[:, lanes]
                    dst[ch * 4 + cl, :, lanes] = piece.astype(BF)

    def spread(n, left, right, twist):
        @pl.loop(0, 4)
        def _(m):
            out = dot(left, right[pl.ds(m * 8, 8)].reshape(256, 512), NT)
            for part in range(2):
                piece = out[:, part * 128 : part * 128 + 128]
                if twist is not None:
                    piece = piece * twist[...]
                lanes = pl.ds(pl.multiple_of(m * 256 + part * 128, 128), 128)
                sbuf[n, :, :, lanes] = piece.astype(BF).reshape(16, 32, 128)

    def share(n, first, second):
        @pl.loop(0, 4)
        def _(m):
            lanes = pl.ds(pl.multiple_of(m * 128, 128), 128)
            out = dot(first[:, :, lanes].reshape(1024, 128), second[...].reshape(1024, 512), TN)
            out = out.astype(BF)
            for p in range(4):
                gb[n, p % 2, m * 2 + p // 2] = out[p * 32 : p * 32 + 32]

    def core_copy(n):
        return remote(gb.at[n, 1 - co], gc.at[n], gcs_sem.at[n], gcr_sem.at[n], CORE)

    def core_send(n):
        core_copy(n).start()

    def blocks_wait(buf, count, ssem, rsem):
        blocks = buf.at[pl.ds(0, count)]
        return remote(blocks, blocks, ssem, rsem, CORE)

    XY = [(dx, dy) for dx in (2, 1, 3, 0) for dy in (2, 1, 3, 0) if dx or dy]
    Z = [(dh, dl) for dh in (2, 1, 3, 0) for dl in range(2) if dh or dl]

    def xy_wait(n):
        return blocks_wait(xr.at[n], 15, xs_sem.at[n], xr_sem.at[n])

    def z_wait(n):
        return blocks_wait(zr.at[n], 7, zs_sem.at[n], zr_sem.at[n])

    def y_wait(n):
        return blocks_wait(yr.at[n], 3, ys_sem.at[n], yr_sem.at[n])

    def xy_send(n):
        core_copy(n).wait_recv()

        @pl.loop(0, 4)
        def _(m):
            total = gb[n, co, pl.ds(m * 2, 2)].astype(F32) + gc[n, pl.ds(m * 2, 2)].astype(F32)
            total = total.astype(BF).reshape(64, 512)
            for p in range(4):
                xs[n, m * 4 + p] = total[:, p * 128 : p * 128 + 128]

        for dx, dy in XY:
            to = ((x + dx) % 4) * 4 + (y + dy) % 4
            remote(
                xs.at[n, to], xr.at[n, x * 4 + y], xs_sem.at[n], xr_sem.at[n],
                device(dx, 0, 0, dy, 0),
            ).start()
        xr[n, x * 4 + y] = xs[n, x * 4 + y]

    def z_send(n):
        xy_wait(n).wait_recv()
        total = xr[n, 0].astype(F32)
        for p in range(1, 16):
            total = total + xr[n, p].astype(F32)
        zb[n] = total.astype(BF).reshape(2, 32, 128)
        for dh, dl in Z:
            remote(
                zb.at[n, (zl + dl) % 2], zr.at[n, zh * 2 + zl], zs_sem.at[n], zr_sem.at[n],
                device(0, dl, 0, 0, dh),
            ).start()
        zr[n, zh * 2 + zl] = zb[n, zl]

    def y_send(n):
        z_wait(n).wait_recv()
        total = zr[n, 0].astype(F32)
        for p in range(1, 8):
            total = total + zr[n, p].astype(F32)
        yr[n, y] = total * SCALE
        for dy in (2, 1, 3):
            remote(
                yr.at[n, y], yr.at[n, y], ys_sem.at[n], yr_sem.at[n], device(0, 0, 0, dy, 0)
            ).start()

    def finish(n):
        y_wait(n).wait_recv()
        for p in range(4):
            grads[n, :, p * 128 : p * 128 + 128] = yr[n, p]

    def reduce_end(n):
        core_copy(n).wait_send()
        xy_wait(n).wait_send()
        z_wait(n).wait_send()
        y_wait(n).wait_send()

    def outputs(left, f, dims, dst):
        @pl.loop(0, 2)
        def _(n):
            rows = pl.ds(pl.multiple_of(n * 16, 16), 16)
            out = dot(left[:, rows, :].reshape(512, 512), factor(f), dims).astype(BF)
            dst[pl.ds(n * 16, 16)] = dot(perm_out[...], out, NN).astype(BF).reshape(16, 32, 512)

    gather_a(R1, True)
    load_wait(0, kn)
    load_wait(1, vn)
    product(kn, vn, wx)
    shuffle(wx, us)
    gather_b(R1, True)
    for copy in twist_loads:
        copy.wait()
    tw1x[...] = jnp.concatenate([tw1t[...]] * 4, axis=0).T
    tw2x[...] = jnp.concatenate([tw2t[...]] * 4, axis=0).T
    gather_c(R1)
    for f in (L2, L1, R2):
        gather_a(f, False)
    gather_d(R1)
    fact[0] = factor(R1).T
    spread(T1, fact[0], us, tw1x)
    for f in (L2, L1, R2):
        gather_b(f, False)
    exchange_send(T1)

    gather_c(L2)
    load_wait(2, gn)
    load_wait(3, qn)
    product(gn, qn, wx)
    shuffle(wx, gos)
    gather_d(L2)
    spread(DT2, factor(L2), gos, None)
    for f in (L1, R2):
        gather_c(f)
    regroup[...] = grid2(
        (512, 512),
        lambda r, q: (r >> 7 == ((q >> 5) & 3)) & (((r >> 5) & 3) == q >> 7) & ((r & 31) == (q & 31)),
    )
    perm_out[...] = grid2((512, 512), lambda q, r: (r >> 4 == (q & 31)) & ((r & 15) == q >> 5))
    load_wait(4, hn)
    shuffle(hn, hs)
    for f in (L1, R2):
        gather_d(f)
    fact[1] = factor(R2).T
    exchange_send(DT2)

    arrange(T1, t1x, None)

    @pl.loop(0, 4)
    def _(m):
        rows = pl.ds(m * 8, 8)
        out = dot(t1x[rows].reshape(256, 512), factor(L1), NN).reshape(8, 32, 512)
        zs[rows] = out
        wx[rows] = (out * hs[rows].astype(F32)).astype(BF)

    spread(T2, fact[1], wx, tw2x)
    exchange_send(T2)

    arrange(DT2, ds2x, tw2t)

    @pl.loop(0, 2)
    def _(n):
        rows = pl.ds(pl.multiple_of(n * 16, 16), 16)
        out = dot(ds2x[:, rows, :].reshape(512, 512), factor(R2), NT).reshape(32, 16, 512)
        dzx[:, rows, :] = (out * hs[:, rows, :].astype(F32)).astype(BF)
        grad = (out * zs[:, rows, :]).astype(BF).reshape(512, 512)
        hn[pl.ds(n * 16, 16)] = dot(perm_out[...], grad, NN).astype(BF).reshape(16, 32, 512)

    spread(DT1, factor(L1), dzx, None)
    store(2, gh_hbm, hn)
    share(GRO, wx, ds2x)
    core_send(GRO)
    share(GLI, t1x, dzx)
    core_send(GLI)
    xy_send(GRO)
    xy_send(GLI)
    exchange_send(DT1)
    z_send(GRO)
    z_send(GLI)

    arrange(T2, t2x, None)
    share(GLO, t2x, gos)
    core_send(GLO)
    outputs(t2x, L2, NN, qn)
    store(0, o_hbm, qn)
    xy_send(GLO)
    y_send(GRO)
    y_send(GLI)
    z_send(GLO)

    arrange(DT1, ds1x, tw1t)
    share(GRI, us, ds1x)
    core_send(GRI)
    y_send(GLO)
    xy_send(GRI)
    outputs(ds1x, R1, NT, kn)
    store(1, du_hbm, kn)
    for n in (GRO, GLI, GLO):
        finish(n)
    z_send(GRI)
    exchange_end()
    gather_end()
    for n in (GRO, GLI, GLO):
        reduce_end(n)
    y_send(GRI)
    for n, vmem in enumerate((qn, kn, hn)):
        store_wait(n, vmem)
    finish(GRI)
    copy = pltpu.make_async_copy(grads, grads_hbm, own_sem.at[0])
    copy.start()
    reduce_end(GRI)
    copy.wait()


def products(
    o_hbm, du_hbm, gh_hbm, grads_hbm, q_hbm, g_hbm, k_hbm, v_hbm,
    mo_out, gq_out, gk_out, gv_out, gh_out, gri_out, gli_out, gro_out, glo_out,
    value, first, second, through, grads, in_sem, out_sem,
):
    lanes = 16384 // PARTS

    def window(ref, p):
        return ref.at[:, pl.ds(p * lanes, lanes)]

    sources = ((o_hbm, q_hbm, g_hbm), (du_hbm, v_hbm, k_hbm))
    targets = ((mo_out, gq_out), (gk_out, gv_out))
    steps = [(s, p) for s in range(2) for p in range(PARTS)]

    def loads(n):
        s, p = steps[n]
        return [
            pltpu.make_async_copy(window(ref, p), buf.at[n], in_sem.at[n, m])
            for m, (ref, buf) in enumerate(zip(sources[s], (value, first, second)))
        ]

    def stores(n):
        s, p = steps[n]
        return [
            pltpu.make_async_copy(buf.at[n], window(ref, p), out_sem.at[n, m])
            for m, (ref, buf) in enumerate(zip(targets[s], (first, second)))
        ]

    extra = len(steps)
    whole_in = [
        pltpu.make_async_copy(gh_hbm, through, in_sem.at[extra, 0]),
        pltpu.make_async_copy(grads_hbm, grads, in_sem.at[extra, 1]),
    ]
    for n in range(len(steps)):
        for copy in loads(n):
            copy.start()
    for copy in whole_in:
        copy.start()
    for n in range(len(steps)):
        for copy in loads(n):
            copy.wait()
        factor = value[n].astype(F32)
        first[n] = (factor * first[n].astype(F32)).astype(BF)
        second[n] = (factor * second[n].astype(F32)).astype(BF)
        for copy in stores(n):
            copy.start()
    for copy in whole_in:
        copy.wait()
    whole_out = [pltpu.make_async_copy(through, gh_out, out_sem.at[extra, 0])] + [
        pltpu.make_async_copy(grads.at[n], ref, out_sem.at[extra + 1 + n // 2, n % 2])
        for n, ref in ((GRI, gri_out), (GLI, gli_out), (GRO, gro_out), (GLO, glo_out))
    ]
    for copy in whole_out:
        copy.start()
    for n in range(len(steps)):
        for copy in stores(n):
            copy.wait()
    for copy in whole_out:
        copy.wait()


def shards(
    query, key, values, kern, cotangent, rin, lin, rout, lout, twiddle_one, twiddle_two
):
    any_spec = pl.BlockSpec(memory_space=pl.ANY)
    stream = pltpu.VMEM((32, 32, 512), BF)
    dma = pltpu.SemaphoreType.DMA
    wide = jax.ShapeDtypeStruct((32, 16384), BF)
    small = jax.ShapeDtypeStruct((32, 512), F32)
    o, du, gh, grads = pl.pallas_call(
        mixer,
        out_shape=[wide] * 3 + [jax.ShapeDtypeStruct((4, 32, 512), F32)],
        in_specs=[any_spec] * 11,
        out_specs=[any_spec] * 4,
        scratch_shapes=[stream] * 5
        + [stream] * 3
        + [pltpu.VMEM((32, 32, 512), F32)]
        + [pltpu.VMEM((4, 16, 32, 512), BF), pltpu.VMEM((2, 512, 512), BF)]
        + [stream] * 6
        + [pltpu.VMEM((4, 16, 32, 1024), BF)] * 2
        + [pltpu.VMEM((512, 512), BF)] * 3
        + [pltpu.VMEM((512, 128), F32)] * 2
        + [pltpu.VMEM((32, 512), F32)] * 2
        + [
            pltpu.VMEM((4, 2, 8, 32, 512), BF),
            pltpu.VMEM((4, 8, 32, 512), BF),
            pltpu.VMEM((4, 16, 64, 128), BF),
            pltpu.VMEM((4, 16, 64, 128), BF),
            pltpu.VMEM((4, 2, 32, 128), BF),
            pltpu.VMEM((4, 8, 32, 128), BF),
            pltpu.VMEM((4, 4, 32, 128), F32),
            pltpu.VMEM((4, 32, 512), F32),
        ]
        + [
            dma((5,)), dma((6,)), dma((3,)),
            dma((1,)), dma((4, 5)), dma((4, 4)), dma((4, 4)),
            dma((4,)), dma((4,)), dma((4,)), dma((4,)), dma((4,)), dma((4,)),
            dma((4,)), dma((4,)),
        ],
        compiler_params=pltpu.CompilerParams(
            collective_id=0, has_side_effects=True, vmem_limit_bytes=60 << 20
        ),
        cost_estimate=pl.CostEstimate(
            flops=13_000_000_000, bytes_accessed=9 << 20, transcendentals=0
        ),
        name="mixer",
    )(
        query, key, values, kern, cotangent, rin, lin, rout, lout,
        twiddle_one.T, twiddle_two.T,
    )
    part = pltpu.VMEM((2 * PARTS, 32, 16384 // PARTS), BF)
    outs = pl.pallas_call(
        products,
        out_shape=[wide] * 5 + [small] * 4,
        in_specs=[any_spec] * 8,
        out_specs=[any_spec] * 9,
        scratch_shapes=[part] * 3
        + [pltpu.VMEM((32, 16384), BF), pltpu.VMEM((4, 32, 512), F32)]
        + [dma((2 * PARTS + 3, 3))] * 2,
        compiler_params=pltpu.CompilerParams(vmem_limit_bytes=60 << 20),
        cost_estimate=pl.CostEstimate(
            flops=4 << 20, bytes_accessed=13 << 20, transcendentals=0
        ),
        name="products",
    )(o, du, gh, grads, query, cotangent, key, values)
    return tuple(outs)


def solution(mesh):
    wide, rows, cols = P("dp", "seq"), P("dp", None), P(None, "seq")
    return jax.shard_map(
        shards,
        mesh=mesh,
        in_specs=(wide,) * 5 + (rows,) * 4 + (cols,) * 2,
        out_specs=(wide,) * 5 + (rows,) * 4,
        check_vma=False,
    )
```

```python
import math

import jax
import jax.numpy as jnp
from jax import lax
from jax.experimental import pallas as pl
from jax.experimental.pallas import tpu as pltpu
from jax.sharding import PartitionSpec as P

C = 512
NB = 512
BS = 512
SCALE = 1.0 / math.sqrt(C * NB)
BF = jnp.bfloat16
F32 = jnp.float32
NT = (((1,), (1,)), ((), ()))
NN = (((1,), (0,)), ((), ()))
TN = (((0,), (0,)), ((), ()))
R1, L2, L1, R2 = 0, 1, 2, 3
T1, DT2, T2, DT1 = 0, 1, 2, 3
GRO, GLI, GLO, GRI = 0, 1, 2, 3
WINDOW = 4
YORDER = (1, 2, 3, 0)
PARTS = 4


def dot(a, b, dims):
    return lax.dot_general(a, b, dims, preferred_element_type=F32)


def mixer(
    q_hbm, k_hbm, v_hbm, h_hbm, g_hbm, rin, lin, rout, lout, tw1_hbm, tw2_hbm,
    o_hbm, du_hbm, gh_hbm, grads_hbm,
    qn, kn, vn, hn, gn,
    us, gos, hs, zs, fac, fact, t1x, wx, ds2x, dzx, t2x, ds1x,
    sbuf, rbuf, perm_in, perm_out, regroup, tw1x, tw2x, tw1t, tw2t,
    gb, gc, xs, xr, zb, zr, yr, grads,
    ut, xst, xrt, ybt, yrt,
    load_sem, own_sem, out_sem, fs_sem, fr_sem, as_sem, ar_sem,
    gcs_sem, gcr_sem, xs_sem, xr_sem, zs_sem, zr_sem, ys_sem, yr_sem,
    tile_sem, xrt_sem,
):
    dp = lax.axis_index("dp")
    me = lax.axis_index("seq")
    x, zl, co = dp // 4, (dp // 2) % 2, dp % 2
    y, zh = me // 4, me % 4

    def device(dx, dl, dc, dy, dh):
        return {
            "dp": ((x + dx) % 4) * 4 + ((zl + dl) % 2) * 2 + (co + dc) % 2,
            "seq": ((y + dy) % 4) * 4 + (zh + dh) % 4,
        }

    def remote(src, dst, ssem, rsem, to):
        return pltpu.make_async_remote_copy(
            src_ref=src, dst_ref=dst, send_sem=ssem, recv_sem=rsem,
            device_id=to, device_id_type=pl.DeviceIdType.MESH,
        )

    def load(n, hbm, vmem):
        @pl.loop(0, 32)
        def _(i):
            pltpu.make_async_copy(
                hbm.at[:, pl.ds(pl.multiple_of(i * 512, 512), 512)], vmem.at[i], load_sem.at[n]
            ).start()

    def load_wait(n, vmem):
        pltpu.make_async_copy(vmem, vmem, load_sem.at[n]).wait()

    def store(n, hbm, vmem, first=0, last=32):
        @pl.loop(first, last)
        def _(i):
            pltpu.make_async_copy(
                vmem.at[i], hbm.at[:, pl.ds(pl.multiple_of(i * 512, 512), 512)], out_sem.at[n]
            ).start()

    def store_wait(n, vmem):
        pltpu.make_async_copy(vmem, vmem, out_sem.at[n]).wait()

    peers = (
        [(0, 0, 0, dy, dh) for dy in range(4) for dh in range(4) if dy or dh]
        + [(dx, 0, 0, dy, 0) for dx in range(1, 4) for dy in range(4)]
        + [(0, 1, 0, 0, dh) for dh in range(4)]
        + [(dx, 1, 0, 0, 0) for dx in range(1, 4)]
        + [(dx, 0, 1, 0, 0) for dx in range(1, 4)]
        + [(0, 0, 1, 0, 0)]
    )
    barrier = pltpu.get_barrier_semaphore()
    for offset in peers:
        pl.semaphore_signal(
            barrier, inc=1, device_id=device(*offset), device_id_type=pl.DeviceIdType.MESH
        )
    own = (rin, lout, lin, rout)
    twist_loads = (
        pltpu.make_async_copy(tw1_hbm, tw1t, own_sem.at[4]),
        pltpu.make_async_copy(tw2_hbm, tw2t, own_sem.at[5]),
    )
    for f in range(4):
        pltpu.make_async_copy(own[f], fac.at[f, dp], own_sem.at[f]).start()
    load(0, k_hbm, kn)
    load(1, v_hbm, vn)
    for copy in twist_loads:
        copy.start()
    load(2, g_hbm, gn)
    load(3, q_hbm, qn)
    load(4, h_hbm, hn)

    def grid2(shape, hold):
        r = lax.broadcasted_iota(jnp.int32, shape, 0)
        q = lax.broadcasted_iota(jnp.int32, shape, 1)
        return jnp.where(hold(r, q), 1.0, 0.0).astype(BF)

    perm_in[...] = grid2((512, 512), lambda r, q: (r >> 4 == (q & 31)) & ((r & 15) == q >> 5))
    pl.semaphore_wait(barrier, len(peers))

    CORE = device(0, 0, 1, 0, 0)
    zblock = x * 4 + (1 - zl) * 2 + co

    def fsend(f, block, slot, to):
        remote(fac.at[f, block], fac.at[f, block], fs_sem.at[0], fr_sem.at[f, slot], to).start()

    def fwait(f, slot, count):
        blocks = fac.at[f, pl.ds(0, count)]
        remote(blocks, blocks, fs_sem.at[0], fr_sem.at[f, slot], CORE).wait_recv()

    def fslot(dx):
        return 1 + dx

    def gather_a(f, direct):
        pltpu.make_async_copy(own[f], fac.at[f, dp], own_sem.at[f]).wait()
        fsend(f, dp, fslot(0), device(0, 1, 0, 0, 0))
        for dx in (2, 1, 3):
            fsend(f, dp, fslot(dx), device(dx, 0, 0, 0, 0))
            if direct:
                fsend(f, dp, fslot(dx), device(dx, 1, 0, 0, 0))
        fsend(f, dp, 0, CORE)

    def gather_b(f, direct):
        fwait(f, fslot(0), 1)
        if not direct:
            for dx in (2, 1, 3):
                fsend(f, zblock, fslot(dx), device(dx, 0, 0, 0, 0))
        fsend(f, zblock, 0, CORE)

    def gather_c(f):
        for dx in (1, 3, 2):
            fwait(f, fslot(dx), 2)
            for side in range(2):
                fsend(f, ((x - dx + 4) % 4) * 4 + side * 2 + co, 0, CORE)

    def gather_d(f):
        fwait(f, 0, 8)

    def gather_end():
        blocks = fac.at[:, pl.ds(0, 15)]
        remote(blocks, blocks, fs_sem.at[0], fr_sem.at[0, 0], CORE).wait_send()

    def factor(f):
        return fac[f].reshape(512, 512)

    def shuffle(src, dst):
        @pl.loop(0, 2)
        def _(n):
            block = src[pl.ds(n * 16, 16)].reshape(512, 512)
            dst[:, pl.ds(pl.multiple_of(n * 16, 16), 16), :] = (
                dot(perm_in[...], block, NN).astype(BF).reshape(32, 16, 512)
            )

    def product(a, b, dst):
        @pl.loop(0, 32)
        def _(i):
            dst[i] = (a[i].astype(F32) * b[i].astype(F32)).astype(BF)

    pending = []

    def exchange_group(dy):
        return [(dy, dh) for dh in (2, 1, 3, 0) if dy or dh]

    def exchange_wait_send(n, dy):
        blocks = sbuf.at[n, pl.ds(0, len(exchange_group(dy)))]
        remote(blocks, blocks, as_sem.at[n, dy], ar_sem.at[n, dy], CORE).wait_send()

    def exchange_send(n):
        rbuf[n, me] = sbuf[n, me]
        for dy in YORDER:
            if len(pending) == WINDOW:
                exchange_wait_send(*pending.pop(0))
            for _, dh in exchange_group(dy):
                to = ((y + dy) % 4) * 4 + (zh + dh) % 4
                remote(
                    sbuf.at[n, to], rbuf.at[n, me], as_sem.at[n, dy], ar_sem.at[n, dy],
                    device(0, 0, 0, dy, dh),
                ).start()
            pending.append((n, dy))

    def exchange_end():
        while pending:
            exchange_wait_send(*pending.pop(0))

    def exchange_wait_recv(n, dy):
        blocks = rbuf.at[n, pl.ds(0, len(exchange_group(dy)))]
        remote(blocks, blocks, as_sem.at[n, dy], ar_sem.at[n, dy], CORE).wait_recv()

    def arrange(n, dst, twist, group=YORDER):
        for dy in group:
            exchange_wait_recv(n, dy)
            yg = (y - dy + 4) % 4
            lhs = jnp.concatenate(
                [
                    jnp.concatenate(
                        [rbuf[n, yg * 4 + b, :, ch * 128 : ch * 128 + 128] for b in range(4)], axis=1
                    )
                    for ch in range(8)
                ],
                axis=0,
            )
            lanes = pl.ds(pl.multiple_of(yg * 128, 128), 128)
            out = dot(lhs, regroup[...], NN)
            for ch in range(8):
                for cl in range(4):
                    piece = out[ch * 32 : ch * 32 + 32, cl * 128 : cl * 128 + 128]
                    if twist is not None:
                        piece = piece * twist[:, lanes]
                    dst[ch * 4 + cl, :, lanes] = piece.astype(BF)

    def spread(n, left, right, twist):
        @pl.loop(0, 4)
        def _(m):
            out = dot(left, right[pl.ds(m * 8, 8)].reshape(256, 512), NT)
            for part in range(2):
                piece = out[:, part * 128 : part * 128 + 128]
                if twist is not None:
                    piece = piece * twist[...]
                lanes = pl.ds(pl.multiple_of(m * 256 + part * 128, 128), 128)
                sbuf[n, :, :, lanes] = piece.astype(BF).reshape(16, 32, 128)

    def share(n, first, second):
        @pl.loop(0, 4)
        def _(m):
            lanes = pl.ds(pl.multiple_of(m * 128, 128), 128)
            out = dot(first[:, :, lanes].reshape(1024, 128), second[...].reshape(1024, 512), TN)
            out = out.astype(BF)
            for p in range(4):
                gb[n, p % 2, m * 2 + p // 2] = out[p * 32 : p * 32 + 32]

    def core_copy(n):
        return remote(gb.at[n, 1 - co], gc.at[n], gcs_sem.at[n], gcr_sem.at[n], CORE)

    def core_send(n):
        core_copy(n).start()

    def blocks_wait(buf, count, ssem, rsem):
        blocks = buf.at[pl.ds(0, count)]
        return remote(blocks, blocks, ssem, rsem, CORE)

    XY = [(dx, dy) for dx in (2, 1, 3, 0) for dy in (2, 1, 3, 0) if dx or dy]
    Z = [(dh, dl) for dh in (2, 1, 3, 0) for dl in range(2) if dh or dl]

    def xy_wait(n):
        return blocks_wait(xr.at[n], 15, xs_sem.at[n], xr_sem.at[n])

    def z_wait(n):
        return blocks_wait(zr.at[n], 7, zs_sem.at[n], zr_sem.at[n])

    def y_wait(n):
        return blocks_wait(yr.at[n], 3, ys_sem.at[n], yr_sem.at[n])

    def xy_send(n):
        core_copy(n).wait_recv()

        @pl.loop(0, 4)
        def _(m):
            total = gb[n, co, pl.ds(m * 2, 2)].astype(F32) + gc[n, pl.ds(m * 2, 2)].astype(F32)
            total = total.astype(BF).reshape(64, 512)
            for p in range(4):
                xs[n, m * 4 + p] = total[:, p * 128 : p * 128 + 128]

        for dx, dy in XY:
            to = ((x + dx) % 4) * 4 + (y + dy) % 4
            remote(
                xs.at[n, to], xr.at[n, x * 4 + y], xs_sem.at[n], xr_sem.at[n],
                device(dx, 0, 0, dy, 0),
            ).start()
        xr[n, x * 4 + y] = xs[n, x * 4 + y]

    def z_send(n):
        xy_wait(n).wait_recv()
        total = xr[n, 0].astype(F32)
        for p in range(1, 16):
            total = total + xr[n, p].astype(F32)
        z_spread(n, total)

    def z_spread(n, total):
        zb[n] = total.astype(BF).reshape(2, 32, 128)
        for dh, dl in Z:
            remote(
                zb.at[n, (zl + dl) % 2], zr.at[n, zh * 2 + zl], zs_sem.at[n], zr_sem.at[n],
                device(0, dl, 0, 0, dh),
            ).start()
        zr[n, zh * 2 + zl] = zb[n, zl]

    def y_send(n):
        z_wait(n).wait_recv()
        total = zr[n, 0].astype(F32)
        for p in range(1, 8):
            total = total + zr[n, p].astype(F32)
        yr[n, y] = total * SCALE
        for dy in (2, 1, 3):
            remote(
                yr.at[n, y], yr.at[n, y], ys_sem.at[n], yr_sem.at[n], device(0, 0, 0, dy, 0)
            ).start()

    def finish(n):
        y_wait(n).wait_recv()
        for p in range(4):
            grads[n, :, p * 128 : p * 128 + 128] = yr[n, p]

    def tile_share(dy):
        lanes = pl.ds(pl.multiple_of(((y - dy + 4) % 4) * 128, 128), 128)
        out = dot(ut[...], ds1x[:, :, lanes].reshape(1024, 128), NN).astype(BF)
        for m in range(16):
            half = (m // 2) % 2 * 32
            xst[dy, m // 4 * 2 + m % 2, half : half + 32] = out[m * 32 : m * 32 + 32]
        for dx, dc in XC:
            to = ((x + dx) % 4) * 2 + (co + dc) % 2
            remote(
                xst.at[dy, to], xrt.at[dy, x * 2 + co], tile_sem.at[1], xrt_sem.at[dy],
                device(dx, 0, dc, 0, 0),
            ).start()
        xrt[dy, x * 2 + co] = xst[dy, x * 2 + co]

    XC = [(dx, dc) for dx in (2, 1, 3, 0) for dc in (1, 0) if dx or dc]

    def tile_x_wait(dy):
        blocks_wait(xrt.at[dy], 7, tile_sem.at[1], xrt_sem.at[dy]).wait_recv()
        total = xrt[dy, 0].astype(F32)
        for p in range(1, 8):
            total = total + xrt[dy, p].astype(F32)
        return total

    def tile_y(dy):
        ybt[dy] = tile_x_wait(dy).astype(BF)
        remote(
            ybt.at[dy], yrt.at[dy], tile_sem.at[2], tile_sem.at[3], device(0, 0, 0, 4 - dy, 0)
        ).start()

    def tile_z():
        total = tile_x_wait(0)
        blocks_wait(yrt, 3, tile_sem.at[2], tile_sem.at[3]).wait_recv()
        for dy in (1, 2, 3):
            total = total + yrt[dy].astype(F32)
        z_spread(GRI, total)

    def tile_end():
        sent = xst.at[:, pl.ds(0, 7)]
        remote(sent, sent, tile_sem.at[1], xrt_sem.at[0], CORE).wait_send()
        blocks_wait(ybt, 3, tile_sem.at[2], tile_sem.at[3]).wait_send()
        z_wait(GRI).wait_send()
        y_wait(GRI).wait_send()

    def reduce_end(n):
        core_copy(n).wait_send()
        xy_wait(n).wait_send()
        z_wait(n).wait_send()
        y_wait(n).wait_send()

    def outputs(left, f, dims, dst, first=0, last=2):
        @pl.loop(first, last)
        def _(n):
            rows = pl.ds(pl.multiple_of(n * 16, 16), 16)
            out = dot(left[:, rows, :].reshape(512, 512), factor(f), dims).astype(BF)
            dst[pl.ds(n * 16, 16)] = dot(perm_out[...], out, NN).astype(BF).reshape(16, 32, 512)

    gather_a(R1, True)
    load_wait(0, kn)
    load_wait(1, vn)
    product(kn, vn, wx)
    shuffle(wx, us)
    gather_b(R1, True)
    for copy in twist_loads:
        copy.wait()
    tw1x[...] = jnp.concatenate([tw1t[...]] * 4, axis=0).T
    tw2x[...] = jnp.concatenate([tw2t[...]] * 4, axis=0).T
    gather_c(R1)
    for f in (L2, L1, R2):
        gather_a(f, False)
    gather_d(R1)
    fact[0] = factor(R1).T
    spread(T1, fact[0], us, tw1x)
    for f in (L2, L1, R2):
        gather_b(f, False)
    exchange_send(T1)

    gather_c(L2)
    load_wait(2, gn)
    load_wait(3, qn)
    product(gn, qn, wx)
    shuffle(wx, gos)
    gather_c(L1)
    gather_c(R2)
    gather_d(L2)
    spread(DT2, factor(L2), gos, None)
    exchange_send(DT2)
    regroup[...] = grid2(
        (512, 512),
        lambda r, q: (r >> 7 == ((q >> 5) & 3)) & (((r >> 5) & 3) == q >> 7) & ((r & 31) == (q & 31)),
    )
    perm_out[...] = grid2((512, 512), lambda q, r: (r >> 4 == (q & 31)) & ((r & 15) == q >> 5))
    load_wait(4, hn)
    shuffle(hn, hs)

    arrange(T1, t1x, None)
    gather_d(L1)

    @pl.loop(0, 4)
    def _(m):
        rows = pl.ds(m * 8, 8)
        out = dot(t1x[rows].reshape(256, 512), factor(L1), NN).reshape(8, 32, 512)
        zs[rows] = out
        wx[rows] = (out * hs[rows].astype(F32)).astype(BF)

    gather_d(R2)
    fact[1] = factor(R2).T
    spread(T2, fact[1], wx, tw2x)
    exchange_send(T2)

    arrange(DT2, ds2x, tw2t)

    @pl.loop(0, 2)
    def _(n):
        rows = pl.ds(pl.multiple_of(n * 16, 16), 16)
        out = dot(ds2x[:, rows, :].reshape(512, 512), factor(R2), NT).reshape(32, 16, 512)
        dzx[:, rows, :] = (out * hs[:, rows, :].astype(F32)).astype(BF)
        grad = (out * zs[:, rows, :]).astype(BF).reshape(512, 512)
        hn[pl.ds(n * 16, 16)] = dot(perm_out[...], grad, NN).astype(BF).reshape(16, 32, 512)

    spread(DT1, factor(L1), dzx, None)
    store(2, gh_hbm, hn)
    share(GRO, wx, ds2x)
    core_send(GRO)
    share(GLI, t1x, dzx)
    core_send(GLI)
    xy_send(GRO)
    xy_send(GLI)
    exchange_send(DT1)
    z_send(GRO)
    z_send(GLI)

    arrange(T2, t2x, None)
    share(GLO, t2x, gos)
    core_send(GLO)
    ut[...] = us[...].reshape(1024, 512).T
    outputs(t2x, L2, NN, qn)
    store(0, o_hbm, qn)
    y_send(GRO)
    y_send(GLI)

    arrange(DT1, ds1x, tw1t, YORDER[:1])
    tile_share(1)
    arrange(DT1, ds1x, tw1t, YORDER[1:2])
    tile_share(2)
    xy_send(GLO)
    arrange(DT1, ds1x, tw1t, YORDER[2:3])
    tile_share(3)
    tile_y(1)
    arrange(DT1, ds1x, tw1t, YORDER[3:])
    tile_share(0)
    tile_y(2)
    tile_y(3)
    z_send(GLO)
    outputs(ds1x, R1, NT, kn, 0, 1)
    tile_z()
    y_send(GLO)
    store(1, du_hbm, kn, 0, 16)
    outputs(ds1x, R1, NT, kn, 1, 2)
    store(1, du_hbm, kn, 16, 32)
    y_send(GRI)
    for n in (GRO, GLI, GLO):
        finish(n)
    exchange_end()
    gather_end()
    for n in (GRO, GLI, GLO):
        reduce_end(n)
    for n, vmem in enumerate((qn, kn, hn)):
        store_wait(n, vmem)
    finish(GRI)
    copy = pltpu.make_async_copy(grads, grads_hbm, own_sem.at[0])
    copy.start()
    tile_end()
    copy.wait()


def products(
    o_hbm, du_hbm, gh_hbm, grads_hbm, q_hbm, g_hbm, k_hbm, v_hbm,
    mo_out, gq_out, gk_out, gv_out, gh_out, gri_out, gli_out, gro_out, glo_out,
    value, first, second, through, grads, in_sem, out_sem,
):
    lanes = 16384 // PARTS

    def window(ref, p):
        return ref.at[:, pl.ds(p * lanes, lanes)]

    sources = ((o_hbm, q_hbm, g_hbm), (du_hbm, v_hbm, k_hbm))
    targets = ((mo_out, gq_out), (gk_out, gv_out))
    steps = [(s, p) for s in range(2) for p in range(PARTS)]

    def loads(n):
        s, p = steps[n]
        return [
            pltpu.make_async_copy(window(ref, p), buf.at[n], in_sem.at[n, m])
            for m, (ref, buf) in enumerate(zip(sources[s], (value, first, second)))
        ]

    def stores(n):
        s, p = steps[n]
        return [
            pltpu.make_async_copy(buf.at[n], window(ref, p), out_sem.at[n, m])
            for m, (ref, buf) in enumerate(zip(targets[s], (first, second)))
        ]

    extra = len(steps)
    whole_in = [
        pltpu.make_async_copy(gh_hbm, through, in_sem.at[extra, 0]),
        pltpu.make_async_copy(grads_hbm, grads, in_sem.at[extra, 1]),
    ]
    for n in range(len(steps)):
        for copy in loads(n):
            copy.start()
    for copy in whole_in:
        copy.start()
    for n in range(len(steps)):
        for copy in loads(n):
            copy.wait()
        factor = value[n].astype(F32)
        first[n] = (factor * first[n].astype(F32)).astype(BF)
        second[n] = (factor * second[n].astype(F32)).astype(BF)
        for copy in stores(n):
            copy.start()
    for copy in whole_in:
        copy.wait()
    whole_out = [pltpu.make_async_copy(through, gh_out, out_sem.at[extra, 0])] + [
        pltpu.make_async_copy(grads.at[n], ref, out_sem.at[extra + 1 + n // 2, n % 2])
        for n, ref in ((GRI, gri_out), (GLI, gli_out), (GRO, gro_out), (GLO, glo_out))
    ]
    for copy in whole_out:
        copy.start()
    for n in range(len(steps)):
        for copy in stores(n):
            copy.wait()
    for copy in whole_out:
        copy.wait()


def shards(
    query, key, values, kern, cotangent, rin, lin, rout, lout, twiddle_one, twiddle_two
):
    any_spec = pl.BlockSpec(memory_space=pl.ANY)
    stream = pltpu.VMEM((32, 32, 512), BF)
    dma = pltpu.SemaphoreType.DMA
    wide = jax.ShapeDtypeStruct((32, 16384), BF)
    small = jax.ShapeDtypeStruct((32, 512), F32)
    o, du, gh, grads = pl.pallas_call(
        mixer,
        out_shape=[wide] * 3 + [jax.ShapeDtypeStruct((4, 32, 512), F32)],
        in_specs=[any_spec] * 11,
        out_specs=[any_spec] * 4,
        scratch_shapes=[stream] * 5
        + [stream] * 3
        + [pltpu.VMEM((32, 32, 512), F32)]
        + [pltpu.VMEM((4, 16, 32, 512), BF), pltpu.VMEM((2, 512, 512), BF)]
        + [stream] * 6
        + [pltpu.VMEM((4, 16, 32, 1024), BF)] * 2
        + [pltpu.VMEM((512, 512), BF)] * 3
        + [pltpu.VMEM((512, 128), F32)] * 2
        + [pltpu.VMEM((32, 512), F32)] * 2
        + [
            pltpu.VMEM((4, 2, 8, 32, 512), BF),
            pltpu.VMEM((4, 8, 32, 512), BF),
            pltpu.VMEM((4, 16, 64, 128), BF),
            pltpu.VMEM((4, 16, 64, 128), BF),
            pltpu.VMEM((4, 2, 32, 128), BF),
            pltpu.VMEM((4, 8, 32, 128), BF),
            pltpu.VMEM((4, 4, 32, 128), F32),
            pltpu.VMEM((4, 32, 512), F32),
            pltpu.VMEM((512, 1024), BF),
            pltpu.VMEM((4, 8, 64, 128), BF),
            pltpu.VMEM((4, 8, 64, 128), BF),
            pltpu.VMEM((4, 64, 128), BF),
            pltpu.VMEM((4, 64, 128), BF),
        ]
        + [
            dma((5,)), dma((6,)), dma((3,)),
            dma((1,)), dma((4, 5)), dma((4, 4)), dma((4, 4)),
            dma((4,)), dma((4,)), dma((4,)), dma((4,)), dma((4,)), dma((4,)),
            dma((4,)), dma((4,)), dma((4,)), dma((4,)),
        ],
        compiler_params=pltpu.CompilerParams(
            collective_id=0, has_side_effects=True, vmem_limit_bytes=60 << 20
        ),
        cost_estimate=pl.CostEstimate(
            flops=13_000_000_000, bytes_accessed=9 << 20, transcendentals=0
        ),
        name="mixer",
    )(
        query, key, values, kern, cotangent, rin, lin, rout, lout,
        twiddle_one.T, twiddle_two.T,
    )
    part = pltpu.VMEM((2 * PARTS, 32, 16384 // PARTS), BF)
    outs = pl.pallas_call(
        products,
        out_shape=[wide] * 5 + [small] * 4,
        in_specs=[any_spec] * 8,
        out_specs=[any_spec] * 9,
        scratch_shapes=[part] * 3
        + [pltpu.VMEM((32, 16384), BF), pltpu.VMEM((4, 32, 512), F32)]
        + [dma((2 * PARTS + 3, 3))] * 2,
        compiler_params=pltpu.CompilerParams(vmem_limit_bytes=60 << 20),
        cost_estimate=pl.CostEstimate(
            flops=4 << 20, bytes_accessed=13 << 20, transcendentals=0
        ),
        name="products",
    )(o, du, gh, grads, query, cotangent, key, values)
    return tuple(outs)


def solution(mesh):
    wide, rows, cols = P("dp", "seq"), P("dp", None), P(None, "seq")
    return jax.shard_map(
        shards,
        mesh=mesh,
        in_specs=(wide,) * 5 + (rows,) * 4 + (cols,) * 2,
        out_specs=(wide,) * 5 + (rows,) * 4,
        check_vma=False,
    )
```
